32 devices in a mesh: seq: 8 (over z, x), head: 4 (over y, core).
Axes of the slice: x: 2, y: 2, z: 4, core: 2. Of those that a mesh axis runs over, the one named last changes fastest.
Arguments:
- layer_input: bfloat16 [2048, 4096], P('seq', 'head'), may hold values from -6 to 6
- value_weight: bfloat16 [4096, 4096], P(None, 'head'), may hold values from -0.09375 to 0.09375
- state_weight: bfloat16 [4096, 2048], P(None, 'head'), may hold values from -0.02734375 to 0.02734375
- output_weight: bfloat16 [4096, 4096], P('head'), may hold values from -0.09375 to 0.09375
- log_decay: float32 [64, 2048], P('head', 'seq'), may hold values from -1.5 to 0, as said below
- skip_gain: float32 [64], P('head'), may hold values from 0.5 to 1.5
- output_grad: bfloat16 [2048, 4096], P('seq', 'head'), may hold values from -6 to 6
Outputs:
- layer_output: bfloat16 [2048, 4096], P('seq', 'head')
- input_grad: bfloat16 [2048, 4096], P('seq', 'head')
The draws below stay inside these ranges and needn't reach their ends.
Inputs may be any that keep to these rules, and one draw needn't show every extreme that they name: `log_decay`: each entry is below zero.
All inputs are finite; a program needn't handle non-finite values.
Results may differ from the reference program's by a relative error of at most 0.015.
Values may be sent and summed in bfloat16 or wider, within the bound.
A program may use at most 64 MiB of HBM per device.

```python
import jax
import jax.numpy as jnp
from jax import lax

D = 4096
MIXER_HEADS = 64
HEAD_DIM = 64
STATE = 128
GROUPS = 8
BLOCK = 256
TOK_DEV = 256
SEQUENCE_TOKENS = 2048
INNER = 4096


def draw_log_decay(key, part):
    random_subkeys = jax.random.split(key, 7)
    fast_share = 0.4
    fast_heads = jax.random.bernoulli(random_subkeys[0], fast_share, (MIXER_HEADS, 1))
    fast_rate = jnp.exp(jax.random.uniform(random_subkeys[1], (MIXER_HEADS, 1), jnp.float32, jnp.log(1.0 / 50.0), jnp.log(1.0 / 30.0)))
    slow_rate = jnp.exp(jax.random.uniform(random_subkeys[2], (MIXER_HEADS, 1), jnp.float32, jnp.log(0.1), jnp.log(0.5))) / SEQUENCE_TOKENS
    blocks = SEQUENCE_TOKENS // TOK_DEV
    factor = jnp.exp(jax.random.uniform(random_subkeys[3], (MIXER_HEADS, blocks, 1), jnp.float32, jnp.log(0.5), jnp.log(1.5)))
    factor = jnp.broadcast_to(factor, (MIXER_HEADS, blocks, TOK_DEV)).reshape(MIXER_HEADS, SEQUENCE_TOKENS)
    roughness = jax.random.uniform(random_subkeys[4], (MIXER_HEADS, SEQUENCE_TOKENS), jnp.float32, 0.5, 1.5)
    decay_speed = jnp.where(fast_heads, fast_rate, slow_rate) * factor * roughness
    positions_list = jax.random.randint(random_subkeys[5], (MIXER_HEADS, 2, 1), 0, SEQUENCE_TOKENS)
    surge_depth = jax.random.uniform(random_subkeys[6], (MIXER_HEADS, 2, 1), jnp.float32, jnp.log(0.5), jnp.log(0.8))
    surge_hits = jnp.arange(SEQUENCE_TOKENS, dtype=jnp.int32)[None, None, :] == positions_list
    surge_total = jnp.sum(jnp.where(surge_hits, surge_depth, 0.0), axis=1)
    return (surge_total - decay_speed).astype(jnp.float32)


def level_of(rng, extent, cuts, least, high):
    factor_of = 1.0
    for dim, shards_of in cuts:
        heights = jax.random.uniform(jax.random.fold_in(jax.random.fold_in(rng, 6), dim), (shards_of,), jnp.float32, least / len(cuts), high / len(cuts))
        factor_of = factor_of * jnp.repeat(jnp.exp(heights), extent[dim] // shards_of).reshape((-1,) + (1,) * (len(extent) - 1 - dim))
    return factor_of


def bell_draw(stream_key, dims, scale, most, cuts=(), kind=jnp.bfloat16):
    drawn = jax.random.normal(stream_key, dims, jnp.float32) * scale
    if len(cuts) > 0:
        drawn = level_of(stream_key, dims, cuts, -0.22, 0.18) * drawn
    return jnp.clip(drawn, min=-most, max=most).astype(kind)


def setup_inputs(seed: int = 0) -> dict:
    splits = jax.random.split(jax.random.key(seed), 8)
    return {
        "layer_input": bell_draw(splits[0], (SEQUENCE_TOKENS, D), 1.0, 6.0, ((0, 8), (1, 4))),
        "value_weight": bell_draw(splits[1], (D, INNER), D ** -0.5, 0.09375, ((1, 4),)),
        "state_weight": bell_draw(splits[2], (D, 2 * STATE * GROUPS), (11 * D) ** -0.5, 0.02734375, ((1, 4),)),
        "output_weight": bell_draw(splits[3], (INNER, D), INNER ** -0.5, 0.09375, ((0, 4),)),
        "log_decay": draw_log_decay(jax.random.fold_in(splits[7], 71), 0),
        "skip_gain": jnp.clip(0.5 + 1.0 * jax.random.uniform(splits[5], (MIXER_HEADS,), jnp.float32) ** level_of(splits[5], (MIXER_HEADS,), ((0, 4),), -0.2, 0.2), 0.5, 1.5),
        "output_grad": bell_draw(splits[6], (SEQUENCE_TOKENS, D), 1.0, 6.0, ((0, 8), (1, 4))),
    }


highest = lax.Precision.HIGHEST

def block_step(carried, pieces):
    values, writer, reader, decays = pieces
    running = jnp.cumsum(decays, axis=-1)
    inflow = jnp.sqrt(-jnp.expm1(2.0 * decays))
    length = decays.shape[-1]
    causal = jnp.arange(length)[:, None] >= jnp.arange(length)[None, :]
    spread = running[..., :, None] - running[..., None, :]
    kernel = jnp.where(causal, jnp.exp(jnp.where(causal, spread, 0.0)), 0.0)
    scores = jnp.einsum('tgn,sgn->gts', reader, writer, precision=highest)
    weights = scores[:, None] * kernel * inflow[..., None, :]
    within = jnp.einsum('ghts,sghp->tghp', weights, values, precision=highest)
    entering = jnp.transpose(jnp.exp(running), (2, 0, 1))[..., None]
    carried_part = jnp.einsum('tgn,ghnp->tghp', reader, carried, precision=highest) * entering
    to_end = jnp.exp(running[..., -1:] - running) * inflow
    fresh_part = jnp.einsum('sgn,ghs,sghp->ghnp', writer, to_end, values, precision=highest)
    carried = jnp.exp(running[..., -1])[..., None, None] * carried + fresh_part
    return (carried, within + carried_part)

def scan_blocks(values, writer, reader, decays, carried, block_rows, step_function):
    total_rows, group_count, per_group, head_width = values.shape
    block_count = total_rows // block_rows
    pieces = (values.reshape(block_count, block_rows, group_count, per_group, head_width), writer.reshape(block_count, block_rows, group_count, writer.shape[-1]), reader.reshape(block_count, block_rows, group_count, reader.shape[-1]), jnp.moveaxis(decays.reshape(group_count, per_group, block_count, block_rows), 2, 0))
    carried, outputs = lax.scan(step_function, carried, pieces)
    return (carried, outputs.reshape(total_rows, group_count, per_group, head_width))

def mixer_pass(value_input, pair_input, log_decay, skip_gain):
    total_rows = value_input.shape[0]
    per_group = MIXER_HEADS // GROUPS
    head_values = value_input.reshape(total_rows, GROUPS, per_group, HEAD_DIM)
    pair_split = pair_input.reshape(total_rows, GROUPS, 2, STATE)
    decays = log_decay.reshape(GROUPS, per_group, total_rows)
    zero_state = jnp.zeros((GROUPS, per_group, STATE, HEAD_DIM), jnp.float32)
    final_state, outputs = scan_blocks(head_values, pair_split[:, :, 0], pair_split[:, :, 1], decays, zero_state, BLOCK, jax.checkpoint(block_step))
    outputs = outputs + skip_gain.reshape(GROUPS, per_group)[None, :, :, None] * head_values
    return outputs.reshape(total_rows, MIXER_HEADS * HEAD_DIM)

def reference(layer_input, value_weight, state_weight, output_weight, log_decay, skip_gain, output_grad):
    values = jnp.dot(layer_input, value_weight, preferred_element_type=jnp.float32).astype(jnp.bfloat16)
    pair_rows = jnp.dot(layer_input, state_weight, preferred_element_type=jnp.float32).astype(jnp.bfloat16)
    values = lax.optimization_barrier(values)
    pair_rows = lax.optimization_barrier(pair_rows)

    def through(value_input, pair_input):
        return mixer_pass(value_input, pair_input, log_decay, skip_gain)
    mixed_full, pullback = jax.vjp(through, values.astype(jnp.float32), pair_rows.astype(jnp.float32))
    mixer_out = mixed_full.astype(jnp.bfloat16)
    layer_output = jnp.dot(mixer_out, output_weight, preferred_element_type=jnp.float32).astype(jnp.bfloat16)
    mixed_grad = jnp.dot(output_grad, output_weight.T, preferred_element_type=jnp.float32).astype(jnp.bfloat16)
    value_grad, pair_grad = pullback(mixed_grad.astype(jnp.float32))
    input_grad = jnp.dot(value_grad.astype(jnp.bfloat16), value_weight.T, preferred_element_type=jnp.float32)
    input_grad = input_grad + jnp.dot(pair_grad.astype(jnp.bfloat16), state_weight.T, preferred_element_type=jnp.float32)
    return (layer_output, input_grad.astype(jnp.bfloat16))
```

```python
import functools

import jax
import jax.numpy as jnp
from jax import lax
from jax.experimental import pallas as pl
from jax.experimental.pallas import tpu as pltpu

STATE = 128
TILE = 256
CHUNKS = 2
SEMS = 128
f32 = jnp.float32
bf16 = jnp.bfloat16
HIGHEST = lax.Precision.HIGHEST
MESH = pl.DeviceIdType.MESH


def nn(a, b, precision=None):
    return lax.dot_general(a, b, (((1,), (0,)), ((), ())), precision=precision, preferred_element_type=f32)


def nt(a, b, precision=None):
    return lax.dot_general(a, b, (((1,), (1,)), ((), ())), precision=precision, preferred_element_type=f32)


def tn(a, b):
    return lax.dot_general(a, b, (((0,), (0,)), ((), ())), preferred_element_type=f32)


def inflow_of(decay):
    twice = 2.0 * decay
    series = 1.0 + twice * (1.0 / 9.0)
    for n in (8, 7, 6, 5, 4, 3, 2):
        series = 1.0 + twice * series * (1.0 / n)
    near = -twice * series
    far = 1.0 - jnp.exp(twice)
    return jnp.sqrt(jnp.where(twice > -0.5, near, far))


def kernel(
    n_head, n_seq,
    x_ref, g_ref, ld_ref, skip_ref, vw_hbm, sw_hbm, ow_hbm,
    out_ref, ing_ref,
    vw, sw, ow, xs, gs, acc_v, acc_p, acc_g, values, pairs, mgrad, mix, dval, dpair,
    ent_x, end_x, run_x, run_r, inf_r, score, dscore, tv, eg,
    total, excl, dtot, dexc, sendb, recvb, sendd, recvd,
    p_send, p_recv, y_send, y_recv, o_send, o_recv, part,
    ssem, rsem, wsem,
):
    rows, width = x_ref.shape
    vwid = vw.shape[1]
    pwid = sw.shape[1]
    heads = ld_ref.shape[0]
    groups = pwid // (2 * STATE)
    gwid = vwid // groups
    hdim = vwid // heads
    pair = 2 * hdim
    chips = n_head // 2
    steps = recvb.shape[1]
    hi = lax.axis_index("head")
    si = lax.axis_index("seq")
    core = lax.rem(hi, 2)
    chip = hi // 2
    partner = chip * 2 + (1 - core)

    def at_chip(j, c):
        return lax.rem(chip + j, chips) * 2 + c

    barrier = pltpu.get_barrier_semaphore()
    peers = [{"head": partner}] + [{"head": at_chip(j, core)} for j in range(1, chips)]
    offsets = set()
    for k in range(steps):
        offsets |= {2**k % n_seq, (n_seq - 2**k) % n_seq}
    offsets.discard(0)
    peers += [{"seq": lax.rem(si + o, n_seq)} for o in sorted(offsets)]

    counter = [0]

    def remote(src, dst, device):
        i = counter[0]
        counter[0] += 1
        return pltpu.make_async_remote_copy(
            src_ref=src, dst_ref=dst, send_sem=ssem.at[i], recv_sem=rsem.at[i],
            device_id=device, device_id_type=MESH,
        )

    order = [hi, partner]
    for j in range(1, chips):
        order += [at_chip(chips - j, core), at_chip(chips - j, 1 - core)]
    wcopies = []
    wcount = 0
    for src in order:
        at = pl.ds(pl.multiple_of(src * width, width), width)
        three = []
        for a, b in (
            (vw_hbm.at[at, :], vw.at[at, :]),
            (sw_hbm.at[at, :], sw.at[at, :]),
            (ow_hbm.at[:, at], ow.at[:, at]),
        ):
            three.append(pltpu.make_async_copy(a, b, wsem.at[wcount]))
            wcount += 1
        wcopies.append(three)
    for three in wcopies:
        three[0].start()
        three[1].start()

    for peer in peers:
        pl.semaphore_signal(barrier, inc=1, device_id=peer, device_id_type=MESH)
    pl.semaphore_wait(barrier, len(peers))

    crow = rows // CHUNKS

    def gather(t_ref, slots):
        own = remote(t_ref, slots.at[hi], {"head": partner})
        far, fwd = [], []
        for k in range(CHUNKS):
            at = pl.ds(k * crow, crow)
            for j in range(1, chips):
                far.append(remote(t_ref.at[at], slots.at[hi, at], {"head": at_chip(j, core)}))
                src = at_chip(chips - j, core)
                fwd.append(remote(slots.at[src, at], slots.at[src, at], {"head": partner}))
        return own, far, fwd

    x_own, x_far, x_fwd = gather(x_ref, xs)
    g_own, g_far, g_fwd = gather(g_ref, gs)
    for c in x_far:
        c.start()
    x_own.start()
    g_own.start()
    for three in wcopies:
        three[2].start()

    decay = ld_ref[...]
    ti = lax.broadcasted_iota(jnp.int32, (rows, rows), 0)
    si_ = lax.broadcasted_iota(jnp.int32, (rows, rows), 1)
    lower = jnp.where(ti >= si_, 1.0, 0.0).astype(f32)
    eye = jnp.where(ti == si_, 1.0, 0.0).astype(f32)
    run_row = nt(decay, lower, HIGHEST)
    run_col = nt(lower, decay, HIGHEST)
    decay_col = nt(eye, decay, HIGHEST)
    inf_row = inflow_of(decay)
    for h in range(heads):
        run_r[h] = run_row[h : h + 1, :]
        inf_r[h] = inf_row[h : h + 1, :]
    col = lax.broadcasted_iota(jnp.int32, (heads, vwid), 1)
    first = lax.broadcasted_iota(jnp.int32, (heads, vwid), 0) * hdim
    spread = jnp.where((col >= first) & (col < first + hdim), 1.0, 0.0).astype(f32)
    run_x[...] = nn(run_col, spread, HIGHEST)
    ent_x[...] = nn(jnp.exp(run_col), spread, HIGHEST)
    to_end = jnp.exp(run_col[rows - 1 : rows, :] - run_col) * inflow_of(decay_col)
    end_x[...] = nn(to_end, spread, HIGHEST)

    def mul_x(src, block, begin):
        @pl.loop(0, vwid // TILE)
        def _(n):
            at = pl.ds(pl.multiple_of(n * TILE, TILE), TILE)
            p = nn(block[...], vw[pl.ds(pl.multiple_of(src * width, width), width), at])
            acc_v[:, at] = p if begin else acc_v[:, at] + p

        @pl.loop(0, pwid // TILE)
        def _(n):
            at = pl.ds(pl.multiple_of(n * TILE, TILE), TILE)
            p = nn(block[...], sw[pl.ds(pl.multiple_of(src * width, width), width), at])
            acc_p[:, at] = p if begin else acc_p[:, at] + p

    def mul_g(src, block, begin):
        @pl.loop(0, vwid // TILE)
        def _(n):
            at = pl.ds(pl.multiple_of(n * TILE, TILE), TILE)
            p = nt(block[...], ow[at, pl.ds(pl.multiple_of(src * width, width), width)])
            acc_g[:, at] = p if begin else acc_g[:, at] + p

    wcopies[0][0].wait()
    wcopies[0][1].wait()
    mul_x(hi, x_ref, True)
    x_own.wait_recv()
    wcopies[1][0].wait()
    wcopies[1][1].wait()
    mul_x(partner, xs.at[partner], False)
    per = chips - 1
    for k in range(CHUNKS):
        for j in range(per):
            x_far[k * per + j].wait_recv()
            x_fwd[k * per + j].start()
            g_far[k * per + j].start()
    wcopies[0][2].wait()
    mul_g(hi, g_ref, True)
    for j in range(per):
        src = at_chip(chips - 1 - j, core)
        for which in (0, 1):
            wcopies[2 + 2 * j + which][0].wait()
            wcopies[2 + 2 * j + which][1].wait()
        mul_x(src, xs.at[src], False)
        for k in range(CHUNKS):
            x_fwd[k * per + j].wait_recv()
        src = at_chip(chips - 1 - j, 1 - core)
        mul_x(src, xs.at[src], False)
    values[...] = acc_v[...].astype(bf16)
    pairs[...] = acc_p[...].astype(bf16)

    copies = []
    for way in (0, 1):
        for k in range(steps):
            hop = 2**k
            to = si + hop if way == 0 else si - hop
            to = lax.rem(to + n_seq, n_seq)
            a = remote(sendb.at[way, k], recvb.at[way, k], {"seq": to})
            b = remote(sendd.at[way, k], recvd.at[way, k], {"seq": to})
            copies.append((a, b))

    def can_send(way, k):
        return si + 2**k < n_seq if way == 0 else si >= 2**k

    def can_recv(way, k):
        return si >= 2**k if way == 0 else si + 2**k < n_seq

    def scan_send(way, k):
        sendb[way, k] = total[way].astype(bf16)
        sendd[way, k] = dtot[way]

        @pl.when(can_send(way, k))
        def _():
            for c in copies[way * steps + k]:
                c.start()

    def scan_take(way, k):
        @pl.when(can_recv(way, k))
        def _():
            for c in copies[way * steps + k]:
                c.wait_recv()
            got = recvb[way, k].astype(f32)
            excl[way] = excl[way] + dexc[way][0:1, :] * got
            if k < steps - 1:
                total[way] = total[way] + dtot[way][0:1, :] * got
                dexc[way] = dexc[way] * recvd[way, k]
                dtot[way] = dtot[way] * recvd[way, k]

        if k < steps - 1:
            scan_send(way, k + 1)

    def scan_begin(way):
        excl[way] = jnp.zeros(excl.shape[1:], f32)
        dexc[way] = jnp.ones(dexc.shape[1:], f32)
        dtot[way] = jnp.broadcast_to(ent_x[rows - 1 : rows, :], dtot.shape[1:])
        if steps > 0:
            scan_send(way, 0)

    tv[...] = (end_x[...] * values[...].astype(f32)).astype(bf16)
    for g in range(groups):
        cols = slice(g * gwid, (g + 1) * gwid)
        w_at = slice(2 * g * STATE, (2 * g + 1) * STATE)
        total[0, :, cols] = tn(pairs[:, w_at], tv[:, cols])
    scan_begin(0)
    for g in range(groups):
        w_at = slice(2 * g * STATE, (2 * g + 1) * STATE)
        r_at = slice((2 * g + 1) * STATE, (2 * g + 2) * STATE)
        score[g] = nt(pairs[:, r_at], pairs[:, w_at])
        dscore[g] = jnp.zeros((rows, rows), f32)

    g_own.wait_recv()
    wcopies[1][2].wait()
    mul_g(partner, gs.at[partner], False)
    for k in range(CHUNKS):
        for j in range(per):
            g_far[k * per + j].wait_recv()
            g_fwd[k * per + j].start()
    for j in range(per):
        src = at_chip(chips - 1 - j, core)
        for which in (0, 1):
            wcopies[2 + 2 * j + which][2].wait()
        mul_g(src, gs.at[src], False)
        for k in range(CHUNKS):
            g_fwd[k * per + j].wait_recv()
        src = at_chip(chips - 1 - j, 1 - core)
        mul_g(src, gs.at[src], False)
    mgrad[...] = acc_g[...].astype(bf16)
    eg[...] = (ent_x[...] * mgrad[...].astype(f32)).astype(bf16)
    for g in range(groups):
        cols = slice(g * gwid, (g + 1) * gwid)
        r_at = slice((2 * g + 1) * STATE, (2 * g + 2) * STATE)
        total[1, :, cols] = tn(pairs[:, r_at], eg[:, cols])
    scan_begin(1)

    per_group = gwid // pair

    def within(begin, end):
        @pl.loop(begin, end)
        def _(i):
            g = i // per_group
            at = pl.ds(pl.multiple_of(i * pair, pair), pair)
            left = lax.broadcasted_iota(jnp.int32, (rows, pair), 1) < hdim
            causal = lax.broadcasted_iota(jnp.int32, (rows, rows), 0) >= lax.broadcasted_iota(
                jnp.int32, (rows, rows), 1
            )
            vp = values[:, at]
            gp = mgrad[:, at]
            gp32 = gp.astype(f32)
            rx = run_x[:, at]
            s = score[g]
            gain = jnp.where(left, skip_ref[2 * i], skip_ref[2 * i + 1])
            outs, grads, ds = [], [], None
            for h in (0, 1):
                rc = rx[:, h * hdim : h * hdim + 1]
                m = jnp.exp(jnp.where(causal, rc - run_r[2 * i + h], -1e30)) * inf_r[2 * i + h]
                w = (s * m).astype(bf16)
                outs.append(nn(w, vp))
                grads.append(tn(w, gp))
                gh = jnp.where(left == (h == 0), gp32, 0.0).astype(bf16)
                d = m * nt(gh, vp)
                ds = d if ds is None else ds + d
            acc_v[:, at] = jnp.where(left, outs[0], outs[1]) + gain * vp.astype(f32)
            acc_g[:, at] = jnp.where(left, grads[0], grads[1]) + gain * gp32
            dscore[g] = dscore[g] + ds

    n_pairs = heads // 2
    done = 0
    for k in range(steps):
        scan_take(0, k)
        nxt = (n_pairs * (k + 1)) // max(steps, 1) if k < steps - 1 else n_pairs
        if k < steps - 1 or done < n_pairs:
            within(done, nxt)
            done = nxt
        if k < steps - 1:
            scan_take(1, k)

    def tiles(partial, dest, use):
        @pl.loop(0, width // TILE)
        def _(n):
            use(pl.ds(pl.multiple_of(n * TILE, TILE), TILE), partial(dest * width + n * TILE))

    def scatter_copies(u):
        near = [
            remote(p_send.at[u, j], p_recv.at[u, j], {"head": partner}) for j in range(per)
        ]
        far = [
            remote(y_send.at[u, j], y_recv.at[u, j], {"head": at_chip(j + 1, core)})
            for j in range(per)
        ]
        own = remote(o_send.at[u], o_recv.at[u], {"head": partner})
        return near, far, own

    def scatter_begin(u, partial):
        near, far, own = scatter_copies(u)
        for j in range(per):
            def keep(at, p):
                p_send[u, j, :, at] = p.astype(bf16)

            tiles(partial, at_chip(j + 1, 1 - core), keep)
            near[j].start()
        for j in range(per):
            def keep_part(at, p):
                part[u, :, at] = p

            tiles(partial, at_chip(j + 1, core), keep_part)
            near[j].wait_recv()
            y_send[u, j] = (part[u] + p_recv[u, j].astype(f32)).astype(bf16)
            far[j].start()

        def keep_own(at, p):
            o_send[u, :, at] = p.astype(bf16)

        tiles(partial, partner, keep_own)
        own.start()

        def keep_mine(at, p):
            part[u, :, at] = p

        tiles(partial, hi, keep_mine)
        return near, far, own

    def scatter_end(u, three, o_ref):
        near, far, own = three
        own.wait_recv()
        s = part[u] + o_recv[u].astype(f32)
        for j in range(per):
            far[j].wait_recv()
            s = s + y_recv[u, j].astype(f32)
        o_ref[...] = s.astype(bf16)
        for c in near + far + [own]:
            c.wait_send()

    for g in range(groups):
        cols = slice(g * gwid, (g + 1) * gwid)
        r_at = slice((2 * g + 1) * STATE, (2 * g + 2) * STATE)
        carried = ent_x[:, cols] * nn(pairs[:, r_at], excl[0, :, cols].astype(bf16))
        mix[:, cols] = (acc_v[:, cols] + carried).astype(bf16)

    def out_partial(first_col):
        return nn(mix[...], ow[:, pl.ds(pl.multiple_of(first_col, TILE), TILE)])

    first_rs = scatter_begin(0, out_partial)

    if steps > 0:
        scan_take(1, steps - 1)
    for g in range(groups):
        cols = slice(g * gwid, (g + 1) * gwid)
        w_at = slice(2 * g * STATE, (2 * g + 1) * STATE)
        r_at = slice((2 * g + 1) * STATE, (2 * g + 2) * STATE)
        inc = excl[0, :, cols].astype(bf16)
        outg = excl[1, :, cols].astype(bf16)
        dval[:, cols] = (acc_g[:, cols] + end_x[:, cols] * nn(pairs[:, w_at], outg)).astype(bf16)
        ds = dscore[g].astype(bf16)
        dpair[:, w_at] = (tn(ds, pairs[:, r_at]) + nt(tv[:, cols], outg)).astype(bf16)
        dpair[:, r_at] = (nn(ds, pairs[:, w_at]) + nt(eg[:, cols], inc)).astype(bf16)

    def in_partial(first_row):
        at = pl.ds(pl.multiple_of(first_row, TILE), TILE)
        return nt(dval[...], vw[at, :]) + nt(dpair[...], sw[at, :])

    second_rs = scatter_begin(1, in_partial)
    scatter_end(0, first_rs, out_ref)
    scatter_end(1, second_rs, ing_ref)

    for c in [x_own, g_own] + x_far + x_fwd + g_far + g_fwd:
        c.wait_send()
    for way in (0, 1):
        for k in range(steps):
            @pl.when(can_send(way, k))
            def _():
                for c in copies[way * steps + k]:
                    c.wait_send()


def per_device(
    n_head, n_seq,
    layer_input, value_weight, state_weight, output_weight, log_decay, skip_gain, output_grad,
):
    rows, width = layer_input.shape
    full, vwid = value_weight.shape
    pwid = state_weight.shape[1]
    heads = log_decay.shape[0]
    groups = pwid // (2 * STATE)
    steps = max(n_seq - 1, 0).bit_length()
    chips = n_head // 2
    per = max(chips - 1, 1)
    vm = pltpu.VMEM
    scratch = [
        vm((full, vwid), bf16), vm((full, pwid), bf16), vm((vwid, full), bf16),
        vm((n_head, rows, width), bf16), vm((n_head, rows, width), bf16),
        vm((rows, vwid), f32), vm((rows, pwid), f32), vm((rows, vwid), f32),
        vm((rows, vwid), bf16), vm((rows, pwid), bf16), vm((rows, vwid), bf16),
        vm((rows, vwid), bf16), vm((rows, vwid), bf16), vm((rows, pwid), bf16),
        vm((rows, vwid), f32), vm((rows, vwid), f32), vm((rows, vwid), f32),
        vm((heads, 1, rows), f32), vm((heads, 1, rows), f32),
        vm((groups, rows, rows), f32), vm((groups, rows, rows), f32),
        vm((rows, vwid), bf16), vm((rows, vwid), bf16),
        vm((2, STATE, vwid), f32), vm((2, STATE, vwid), f32),
        vm((2, 8, vwid), f32), vm((2, 8, vwid), f32),
        vm((2, steps, STATE, vwid), bf16), vm((2, steps, STATE, vwid), bf16),
        vm((2, steps, 8, vwid), f32), vm((2, steps, 8, vwid), f32),
        vm((2, per, rows, width), bf16), vm((2, per, rows, width), bf16),
        vm((2, per, rows, width), bf16), vm((2, per, rows, width), bf16),
        vm((2, rows, width), bf16), vm((2, rows, width), bf16),
        vm((2, rows, width), f32),
        pltpu.SemaphoreType.DMA((SEMS,)),
        pltpu.SemaphoreType.DMA((SEMS,)),
        pltpu.SemaphoreType.DMA((3 * n_head,)),
    ]
    vspec = pl.BlockSpec(memory_space=vm)
    anys = pl.BlockSpec(memory_space=pl.ANY)
    flops = 2 * rows * full * (3 * vwid + pwid) + 2 * rows * full * (vwid + pwid)
    return pl.pallas_call(
        functools.partial(kernel, n_head, n_seq),
        out_shape=(
            jax.ShapeDtypeStruct((rows, width), bf16),
            jax.ShapeDtypeStruct((rows, width), bf16),
        ),
        in_specs=[vspec, vspec, vspec, pl.BlockSpec(memory_space=pltpu.SMEM), anys, anys, anys],
        out_specs=(vspec, vspec),
        scratch_shapes=scratch,
        compiler_params=pltpu.CompilerParams(
            collective_id=0, has_side_effects=True, vmem_limit_bytes=60 * 2**20
        ),
        cost_estimate=pl.CostEstimate(
            flops=flops, bytes_accessed=2 * full * (2 * vwid + pwid), transcendentals=0
        ),
    )(layer_input, output_grad, log_decay, skip_gain, value_weight, state_weight, output_weight)


def solution(mesh):
    from jax.sharding import PartitionSpec as P

    in_specs = (
        P("seq", "head"),
        P(None, "head"),
        P(None, "head"),
        P("head", None),
        P("head", "seq"),
        P("head"),
        P("seq", "head"),
    )
    out_specs = (P("seq", "head"), P("seq", "head"))
    return jax.shard_map(
        functools.partial(per_device, mesh.shape["head"], mesh.shape["seq"]),
        mesh=mesh, in_specs=in_specs, out_specs=out_specs, check_vma=False,
    )
```

```python
import functools

import jax
import jax.numpy as jnp
from jax import lax
from jax.experimental import pallas as pl
from jax.experimental.pallas import tpu as pltpu

STATE = 128
TILE = 256
CHUNKS = 2
f32 = jnp.float32
bf16 = jnp.bfloat16
HIGHEST = lax.Precision.HIGHEST
MESH = pl.DeviceIdType.MESH


def nn(a, b, precision=None):
    return lax.dot_general(a, b, (((1,), (0,)), ((), ())), precision=precision, preferred_element_type=f32)


def nt(a, b, precision=None):
    return lax.dot_general(a, b, (((1,), (1,)), ((), ())), precision=precision, preferred_element_type=f32)


def tn(a, b):
    return lax.dot_general(a, b, (((0,), (0,)), ((), ())), preferred_element_type=f32)


def inflow_of(decay):
    twice = 2.0 * decay
    series = 1.0 + twice * (1.0 / 9.0)
    for n in (8, 7, 6, 5, 4, 3, 2):
        series = 1.0 + twice * series * (1.0 / n)
    near = -twice * series
    far = 1.0 - jnp.exp(twice)
    return jnp.sqrt(jnp.where(twice > -0.5, near, far))


def kernel(
    n_head, n_seq,
    x_ref, g_ref, ld_ref, skip_ref, vw_hbm, sw_hbm, ow_hbm,
    out_ref, ing_ref,
    vw, sw, ow, xs, gs, acc_v, acc_p, acc_g, values, pairs, mgrad, mix, dval, dpair,
    ent_x, end_x, run_x, run_r, inf_r, score, dscore, tv, eg,
    total, excl, sendb, recvb, backb, backr, sendd, recvd, dec,
    p_send, p_recv, y_send, y_recv, o_send, o_recv, part,
    ssem, rsem, wsem,
):
    rows, width = x_ref.shape
    vwid = vw.shape[1]
    pwid = sw.shape[1]
    heads = ld_ref.shape[0]
    groups = pwid // (2 * STATE)
    gwid = vwid // groups
    hdim = vwid // heads
    pair = 2 * hdim
    chips = n_head // 2
    row_cuts = min(n_seq, STATE // 16)
    col_cuts = n_seq // row_cuts
    prow, pcol = STATE // row_cuts, vwid // col_cuts
    hi = lax.axis_index("head")
    si = lax.axis_index("seq")
    core = lax.rem(hi, 2)
    chip = hi // 2
    partner = chip * 2 + (1 - core)

    def at_chip(j, c):
        return lax.rem(chip + j, chips) * 2 + c

    barrier = pltpu.get_barrier_semaphore()
    peers = [{"head": partner}] + [{"head": at_chip(j, core)} for j in range(1, chips)]
    peers += [{"seq": lax.rem(si + o, n_seq)} for o in range(1, n_seq)]

    counter = [0]

    def remote(src, dst, device):
        i = counter[0]
        counter[0] += 1
        return pltpu.make_async_remote_copy(
            src_ref=src, dst_ref=dst, send_sem=ssem.at[i], recv_sem=rsem.at[i],
            device_id=device, device_id_type=MESH,
        )

    order = [hi, partner]
    for j in range(1, chips):
        order += [at_chip(chips - j, core), at_chip(chips - j, 1 - core)]
    wcopies = []
    wcount = 0
    for src in order:
        at = pl.ds(pl.multiple_of(src * width, width), width)
        three = []
        for a, b in (
            (vw_hbm.at[at, :], vw.at[at, :]),
            (sw_hbm.at[at, :], sw.at[at, :]),
            (ow_hbm.at[:, at], ow.at[:, at]),
        ):
            three.append(pltpu.make_async_copy(a, b, wsem.at[wcount]))
            wcount += 1
        wcopies.append(three)
    for three in wcopies:
        three[0].start()
        three[1].start()

    for peer in peers:
        pl.semaphore_signal(barrier, inc=1, device_id=peer, device_id_type=MESH)
    pl.semaphore_wait(barrier, len(peers))

    crow = rows // CHUNKS

    def gather(t_ref, slots):
        own = remote(t_ref, slots.at[hi], {"head": partner})
        far, fwd = [], []
        for k in range(CHUNKS):
            at = pl.ds(k * crow, crow)
            for j in range(1, chips):
                far.append(remote(t_ref.at[at], slots.at[hi, at], {"head": at_chip(j, core)}))
                src = at_chip(chips - j, core)
                fwd.append(remote(slots.at[src, at], slots.at[src, at], {"head": partner}))
        return own, far, fwd

    x_own, x_far, x_fwd = gather(x_ref, xs)
    g_own, g_far, g_fwd = gather(g_ref, gs)
    for c in x_far:
        c.start()
    x_own.start()
    g_own.start()
    for three in wcopies:
        three[2].start()

    decay = ld_ref[...]
    ti = lax.broadcasted_iota(jnp.int32, (rows, rows), 0)
    si_ = lax.broadcasted_iota(jnp.int32, (rows, rows), 1)
    lower = jnp.where(ti >= si_, 1.0, 0.0).astype(f32)
    eye = jnp.where(ti == si_, 1.0, 0.0).astype(f32)
    run_row = nt(decay, lower, HIGHEST)
    run_col = nt(lower, decay, HIGHEST)
    decay_col = nt(eye, decay, HIGHEST)
    inf_row = inflow_of(decay)
    for h in range(heads):
        run_r[h] = run_row[h : h + 1, :]
        inf_r[h] = inf_row[h : h + 1, :]
    col = lax.broadcasted_iota(jnp.int32, (heads, vwid), 1)
    first = lax.broadcasted_iota(jnp.int32, (heads, vwid), 0) * hdim
    spread = jnp.where((col >= first) & (col < first + hdim), 1.0, 0.0).astype(f32)
    run_x[...] = nn(run_col, spread, HIGHEST)
    ent_x[...] = nn(jnp.exp(run_col), spread, HIGHEST)
    to_end = jnp.exp(run_col[rows - 1 : rows, :] - run_col) * inflow_of(decay_col)
    end_x[...] = nn(to_end, spread, HIGHEST)

    sendd[...] = jnp.zeros(sendd.shape, f32)
    sendd[:, 0:heads] = jnp.broadcast_to(jnp.exp(run_col[rows - 1 : rows, :]), (8, heads))
    recvd[si] = sendd[...]
    d_copies = [
        remote(sendd, recvd.at[si], {"seq": lax.rem(si + o, n_seq)}) for o in range(1, n_seq)
    ]
    for c in d_copies:
        c.start()

    def mul_x(src, block, begin):
        @pl.loop(0, vwid // TILE)
        def _(n):
            at = pl.ds(pl.multiple_of(n * TILE, TILE), TILE)
            p = nn(block[...], vw[pl.ds(pl.multiple_of(src * width, width), width), at])
            acc_v[:, at] = p if begin else acc_v[:, at] + p

        @pl.loop(0, pwid // TILE)
        def _(n):
            at = pl.ds(pl.multiple_of(n * TILE, TILE), TILE)
            p = nn(block[...], sw[pl.ds(pl.multiple_of(src * width, width), width), at])
            acc_p[:, at] = p if begin else acc_p[:, at] + p

    def mul_g(src, block, begin):
        @pl.loop(0, vwid // TILE)
        def _(n):
            at = pl.ds(pl.multiple_of(n * TILE, TILE), TILE)
            p = nt(block[...], ow[at, pl.ds(pl.multiple_of(src * width, width), width)])
            acc_g[:, at] = p if begin else acc_g[:, at] + p

    wcopies[0][0].wait()
    wcopies[0][1].wait()
    mul_x(hi, x_ref, True)
    x_own.wait_recv()
    wcopies[1][0].wait()
    wcopies[1][1].wait()
    mul_x(partner, xs.at[partner], False)
    per = chips - 1
    for k in range(CHUNKS):
        for j in range(per):
            x_far[k * per + j].wait_recv()
            x_fwd[k * per + j].start()
            g_far[k * per + j].start()
    wcopies[0][2].wait()
    mul_g(hi, g_ref, True)
    for j in range(per):
        src = at_chip(chips - 1 - j, core)
        for which in (0, 1):
            wcopies[2 + 2 * j + which][0].wait()
            wcopies[2 + 2 * j + which][1].wait()
        mul_x(src, xs.at[src], False)
        for k in range(CHUNKS):
            x_fwd[k * per + j].wait_recv()
        src = at_chip(chips - 1 - j, 1 - core)
        mul_x(src, xs.at[src], False)
    values[...] = acc_v[...].astype(bf16)
    pairs[...] = acc_p[...].astype(bf16)

    there, back = [], []
    for way in (0, 1):
        to = [lax.rem(si + o, n_seq) for o in range(1, n_seq)]
        there.append([remote(sendb.at[way, t], recvb.at[way, si], {"seq": t}) for t in to])
        back.append([remote(backb.at[way, t], backr.at[way, si], {"seq": t}) for t in to])

    def piece(r):
        row, col = (r % row_cuts) * prow, (r // row_cuts) * pcol
        return slice(row, row + prow), slice(col, col + pcol)

    def scan_begin(way):
        for r in range(n_seq):
            at = piece(r)
            sendb[way, r] = total[way, at[0], at[1]].astype(bf16)
        for c in there[way]:
            c.start()
        recvb[way, si] = sendb[way, si]

    def scan_mid(way):
        for c in there[way]:
            c.wait_recv()
        cols = pl.ds(pl.multiple_of((si // row_cuts) * pcol, 128), pcol)
        state = jnp.zeros((prow, pcol), f32)
        for q in range(n_seq) if way == 0 else range(n_seq - 1, -1, -1):
            backb[way, q] = state.astype(bf16)
            state = dec[q, 0:1, cols] * state + recvb[way, q].astype(f32)
        for c in back[way]:
            c.start()
        backr[way, si] = backb[way, si]

    def scan_end(way):
        for c in back[way]:
            c.wait_recv()
        for r in range(n_seq):
            at = piece(r)
            excl[way, at[0], at[1]] = backr[way, r]

    tv[...] = (end_x[...] * values[...].astype(f32)).astype(bf16)
    for g in range(groups):
        cols = slice(g * gwid, (g + 1) * gwid)
        w_at = slice(2 * g * STATE, (2 * g + 1) * STATE)
        total[0, :, cols] = tn(pairs[:, w_at], tv[:, cols])
    scan_begin(0)
    for c in d_copies:
        c.wait_recv()
    lane = lax.broadcasted_iota(jnp.int32, (128, vwid), 1)
    head = lax.broadcasted_iota(jnp.int32, (128, vwid), 0) * hdim
    widen = jnp.where((lane >= head) & (lane < head + hdim), 1.0, 0.0).astype(f32)
    wide = nn(recvd[...].reshape(n_seq * 8, 128), widen, HIGHEST)
    dec[...] = wide.reshape(n_seq, 8, vwid)
    for g in range(groups):
        w_at = slice(2 * g * STATE, (2 * g + 1) * STATE)
        r_at = slice((2 * g + 1) * STATE, (2 * g + 2) * STATE)
        score[g] = nt(pairs[:, r_at], pairs[:, w_at])
        dscore[g] = jnp.zeros((rows, rows), f32)

    g_own.wait_recv()
    wcopies[1][2].wait()
    mul_g(partner, gs.at[partner], False)
    scan_mid(0)
    for k in range(CHUNKS):
        for j in range(per):
            g_far[k * per + j].wait_recv()
            g_fwd[k * per + j].start()
    for j in range(per):
        src = at_chip(chips - 1 - j, core)
        for which in (0, 1):
            wcopies[2 + 2 * j + which][2].wait()
        mul_g(src, gs.at[src], False)
        for k in range(CHUNKS):
            g_fwd[k * per + j].wait_recv()
        src = at_chip(chips - 1 - j, 1 - core)
        mul_g(src, gs.at[src], False)
    mgrad[...] = acc_g[...].astype(bf16)
    eg[...] = (ent_x[...] * mgrad[...].astype(f32)).astype(bf16)
    for g in range(groups):
        cols = slice(g * gwid, (g + 1) * gwid)
        r_at = slice((2 * g + 1) * STATE, (2 * g + 2) * STATE)
        total[1, :, cols] = tn(pairs[:, r_at], eg[:, cols])
    scan_begin(1)

    per_group = gwid // pair

    def within(begin, end):
        @pl.loop(begin, end)
        def _(i):
            g = i // per_group
            at = pl.ds(pl.multiple_of(i * pair, pair), pair)
            left = lax.broadcasted_iota(jnp.int32, (rows, pair), 1) < hdim
            causal = lax.broadcasted_iota(jnp.int32, (rows, rows), 0) >= lax.broadcasted_iota(
                jnp.int32, (rows, rows), 1
            )
            vp = values[:, at]
            gp = mgrad[:, at]
            gp32 = gp.astype(f32)
            rx = run_x[:, at]
            s = score[g]
            gain = jnp.where(left, skip_ref[2 * i], skip_ref[2 * i + 1])
            outs, grads, ds = [], [], None
            for h in (0, 1):
                rc = rx[:, h * hdim : h * hdim + 1]
                m = jnp.exp(jnp.where(causal, rc - run_r[2 * i + h], -1e30)) * inf_r[2 * i + h]
                w = (s * m).astype(bf16)
                outs.append(nn(w, vp))
                grads.append(tn(w, gp))
                gh = jnp.where(left == (h == 0), gp32, 0.0).astype(bf16)
                d = m * nt(gh, vp)
                ds = d if ds is None else ds + d
            acc_v[:, at] = jnp.where(left, outs[0], outs[1]) + gain * vp.astype(f32)
            acc_g[:, at] = jnp.where(left, grads[0], grads[1]) + gain * gp32
            dscore[g] = dscore[g] + ds

    within(0, heads // 2)
    scan_end(0)

    def tiles(partial, dest, use):
        @pl.loop(0, width // TILE)
        def _(n):
            use(pl.ds(pl.multiple_of(n * TILE, TILE), TILE), partial(dest * width + n * TILE))

    def scatter_copies(u):
        near = [
            remote(p_send.at[u, j], p_recv.at[u, j], {"head": partner}) for j in range(per)
        ]
        far = [
            remote(y_send.at[u, j], y_recv.at[u, j], {"head": at_chip(j + 1, core)})
            for j in range(per)
        ]
        own = remote(o_send.at[u], o_recv.at[u], {"head": partner})
        return near, far, own

    def scatter_begin(u, partial):
        near, far, own = scatter_copies(u)
        for j in range(per):
            def keep(at, p):
                p_send[u, j, :, at] = p.astype(bf16)

            tiles(partial, at_chip(j + 1, 1 - core), keep)
            near[j].start()
        for j in range(per):
            def keep_part(at, p):
                part[u, :, at] = p

            tiles(partial, at_chip(j + 1, core), keep_part)
            near[j].wait_recv()
            y_send[u, j] = (part[u] + p_recv[u, j].astype(f32)).astype(bf16)
            far[j].start()

        def keep_own(at, p):
            o_send[u, :, at] = p.astype(bf16)

        tiles(partial, partner, keep_own)
        own.start()

        def keep_mine(at, p):
            part[u, :, at] = p

        tiles(partial, hi, keep_mine)
        return near, far, own

    def scatter_end(u, three, o_ref):
        near, far, own = three
        own.wait_recv()
        s = part[u] + o_recv[u].astype(f32)
        for j in range(per):
            far[j].wait_recv()
            s = s + y_recv[u, j].astype(f32)
        o_ref[...] = s.astype(bf16)
        for c in near + far + [own]:
            c.wait_send()

    for g in range(groups):
        cols = slice(g * gwid, (g + 1) * gwid)
        r_at = slice((2 * g + 1) * STATE, (2 * g + 2) * STATE)
        carried = ent_x[:, cols] * nn(pairs[:, r_at], excl[0, :, cols])
        mix[:, cols] = (acc_v[:, cols] + carried).astype(bf16)

    def out_partial(first_col):
        return nn(mix[...], ow[:, pl.ds(pl.multiple_of(first_col, TILE), TILE)])

    first_rs = scatter_begin(0, out_partial)

    scan_mid(1)
    scan_end(1)
    for g in range(groups):
        cols = slice(g * gwid, (g + 1) * gwid)
        w_at = slice(2 * g * STATE, (2 * g + 1) * STATE)
        r_at = slice((2 * g + 1) * STATE, (2 * g + 2) * STATE)
        inc = excl[0, :, cols]
        outg = excl[1, :, cols]
        dval[:, cols] = (acc_g[:, cols] + end_x[:, cols] * nn(pairs[:, w_at], outg)).astype(bf16)
        ds = dscore[g].astype(bf16)
        dpair[:, w_at] = (tn(ds, pairs[:, r_at]) + nt(tv[:, cols], outg)).astype(bf16)
        dpair[:, r_at] = (nn(ds, pairs[:, w_at]) + nt(eg[:, cols], inc)).astype(bf16)

    def in_partial(first_row):
        at = pl.ds(pl.multiple_of(first_row, TILE), TILE)
        return nt(dval[...], vw[at, :]) + nt(dpair[...], sw[at, :])

    second_rs = scatter_begin(1, in_partial)
    scatter_end(0, first_rs, out_ref)
    scatter_end(1, second_rs, ing_ref)

    for c in [x_own, g_own] + x_far + x_fwd + g_far + g_fwd:
        c.wait_send()
    for c in d_copies + there[0] + there[1] + back[0] + back[1]:
        c.wait_send()


def per_device(
    n_head, n_seq,
    layer_input, value_weight, state_weight, output_weight, log_decay, skip_gain, output_grad,
):
    rows, width = layer_input.shape
    full, vwid = value_weight.shape
    pwid = state_weight.shape[1]
    heads = log_decay.shape[0]
    groups = pwid // (2 * STATE)
    row_cuts = min(n_seq, STATE // 16)
    piece = (n_seq, STATE // row_cuts, vwid // (n_seq // row_cuts))
    sems = 32 * n_head + 5 * n_seq
    chips = n_head // 2
    per = max(chips - 1, 1)
    vm = pltpu.VMEM
    scratch = [
        vm((full, vwid), bf16), vm((full, pwid), bf16), vm((vwid, full), bf16),
        vm((n_head, rows, width), bf16), vm((n_head, rows, width), bf16),
        vm((rows, vwid), f32), vm((rows, pwid), f32), vm((rows, vwid), f32),
        vm((rows, vwid), bf16), vm((rows, pwid), bf16), vm((rows, vwid), bf16),
        vm((rows, vwid), bf16), vm((rows, vwid), bf16), vm((rows, pwid), bf16),
        vm((rows, vwid), f32), vm((rows, vwid), f32), vm((rows, vwid), f32),
        vm((heads, 1, rows), f32), vm((heads, 1, rows), f32),
        vm((groups, rows, rows), f32), vm((groups, rows, rows), f32),
        vm((rows, vwid), bf16), vm((rows, vwid), bf16),
        vm((2, STATE, vwid), f32), vm((2, STATE, vwid), bf16),
        vm((2,) + piece, bf16), vm((2,) + piece, bf16),
        vm((2,) + piece, bf16), vm((2,) + piece, bf16),
        vm((8, 128), f32), vm((n_seq, 8, 128), f32), vm((n_seq, 8, vwid), f32),
        vm((2, per, rows, width), bf16), vm((2, per, rows, width), bf16),
        vm((2, per, rows, width), bf16), vm((2, per, rows, width), bf16),
        vm((2, rows, width), bf16), vm((2, rows, width), bf16),
        vm((2, rows, width), f32),
        pltpu.SemaphoreType.DMA((sems,)),
        pltpu.SemaphoreType.DMA((sems,)),
        pltpu.SemaphoreType.DMA((3 * n_head,)),
    ]
    vspec = pl.BlockSpec(memory_space=vm)
    anys = pl.BlockSpec(memory_space=pl.ANY)
    flops = 2 * rows * full * (3 * vwid + pwid) + 2 * rows * full * (vwid + pwid)
    return pl.pallas_call(
        functools.partial(kernel, n_head, n_seq),
        out_shape=(
            jax.ShapeDtypeStruct((rows, width), bf16),
            jax.ShapeDtypeStruct((rows, width), bf16),
        ),
        in_specs=[vspec, vspec, vspec, pl.BlockSpec(memory_space=pltpu.SMEM), anys, anys, anys],
        out_specs=(vspec, vspec),
        scratch_shapes=scratch,
        compiler_params=pltpu.CompilerParams(
            collective_id=0, has_side_effects=True, vmem_limit_bytes=60 * 2**20
        ),
        cost_estimate=pl.CostEstimate(
            flops=flops, bytes_accessed=2 * full * (2 * vwid + pwid), transcendentals=0
        ),
    )(layer_input, output_grad, log_decay, skip_gain, value_weight, state_weight, output_weight)


def solution(mesh):
    from jax.sharding import PartitionSpec as P

    in_specs = (
        P("seq", "head"),
        P(None, "head"),
        P(None, "head"),
        P("head", None),
        P("head", "seq"),
        P("head"),
        P("seq", "head"),
    )
    out_specs = (P("seq", "head"), P("seq", "head"))
    return jax.shard_map(
        functools.partial(per_device, mesh.shape["head"], mesh.shape["seq"]),
        mesh=mesh, in_specs=in_specs, out_specs=out_specs, check_vma=False,
    )
```

```python
import functools

import jax
import jax.numpy as jnp
from jax import lax
from jax.experimental import pallas as pl
from jax.experimental.pallas import tpu as pltpu

STATE = 128
TILE = 256
CHUNKS = 2
f32 = jnp.float32
bf16 = jnp.bfloat16
HIGHEST = lax.Precision.HIGHEST
MESH = pl.DeviceIdType.MESH


def nn(a, b, precision=None):
    return lax.dot_general(a, b, (((1,), (0,)), ((), ())), precision=precision, preferred_element_type=f32)


def nt(a, b, precision=None):
    return lax.dot_general(a, b, (((1,), (1,)), ((), ())), precision=precision, preferred_element_type=f32)


def tn(a, b):
    return lax.dot_general(a, b, (((0,), (0,)), ((), ())), preferred_element_type=f32)


def inflow_of(decay):
    twice = 2.0 * decay
    series = 1.0 + twice * (1.0 / 9.0)
    for n in (8, 7, 6, 5, 4, 3, 2):
        series = 1.0 + twice * series * (1.0 / n)
    near = -twice * series
    far = 1.0 - jnp.exp(twice)
    return jnp.sqrt(jnp.where(twice > -0.5, near, far))


def kernel(
    n_head, n_seq,
    x_ref, g_ref, ld_ref, skip_ref, vw_hbm, sw_hbm, ow_hbm,
    out_ref, ing_ref,
    vw, sw, ow, xs, gs, acc_v, acc_p, acc_g, values, pairs, mgrad, mix, dval, dpair,
    ent_x, end_x, run_x, run_r, inf_r, score, dscore, tv, eg,
    total, excl, sendb, recvb, backb, backr, sendd, recvd, dec,
    p_send, p_recv, y_send, y_recv, o_send, o_recv, part,
    weight, mask, ssem, rsem, wsem,
):
    rows, width = x_ref.shape
    vwid = vw.shape[1]
    pwid = sw.shape[1]
    heads = ld_ref.shape[0]
    groups = pwid // (2 * STATE)
    gwid = vwid // groups
    hdim = vwid // heads
    pair = 2 * hdim
    chips = n_head // 2
    row_cuts = min(n_seq, STATE // 16)
    col_cuts = n_seq // row_cuts
    prow, pcol = STATE // row_cuts, vwid // col_cuts
    hi = lax.axis_index("head")
    si = lax.axis_index("seq")
    core = lax.rem(hi, 2)
    chip = hi // 2
    partner = chip * 2 + (1 - core)

    def at_chip(j, c):
        return lax.rem(chip + j, chips) * 2 + c

    barrier = pltpu.get_barrier_semaphore()
    peers = [{"head": partner}] + [{"head": at_chip(j, core)} for j in range(1, chips)]
    peers += [{"seq": lax.rem(si + o, n_seq)} for o in range(1, n_seq)]

    counter = [0]

    def remote(src, dst, device):
        i = counter[0]
        counter[0] += 1
        return pltpu.make_async_remote_copy(
            src_ref=src, dst_ref=dst, send_sem=ssem.at[i], recv_sem=rsem.at[i],
            device_id=device, device_id_type=MESH,
        )

    order = [hi, partner]
    for j in range(1, chips):
        order += [at_chip(chips - j, core), at_chip(chips - j, 1 - core)]
    wcopies = []
    wcount = 0
    for src in order:
        at = pl.ds(pl.multiple_of(src * width, width), width)
        three = []
        for a, b in (
            (vw_hbm.at[at, :], vw.at[at, :]),
            (sw_hbm.at[at, :], sw.at[at, :]),
            (ow_hbm.at[:, at], ow.at[:, at]),
        ):
            three.append(pltpu.make_async_copy(a, b, wsem.at[wcount]))
            wcount += 1
        wcopies.append(three)
    x_here = pltpu.make_async_copy(x_ref, xs.at[hi], wsem.at[wcount])
    g_here = pltpu.make_async_copy(g_ref, gs.at[hi], wsem.at[wcount + 1])
    for peer in peers:
        pl.semaphore_signal(barrier, inc=1, device_id=peer, device_id_type=MESH)
    x_here.start()
    for three in wcopies:
        three[0].start()
        three[1].start()
    g_here.start()
    pl.semaphore_wait(barrier, len(peers))

    crow = rows // CHUNKS

    def gather(t_ref, slots):
        own = remote(t_ref, slots.at[hi], {"head": partner})
        far, fwd = [], []
        for k in range(CHUNKS):
            at = pl.ds(k * crow, crow)
            for j in range(1, chips):
                far.append(remote(t_ref.at[at], slots.at[hi, at], {"head": at_chip(j, core)}))
                src = at_chip(chips - j, core)
                fwd.append(remote(slots.at[src, at], slots.at[src, at], {"head": partner}))
        return own, far, fwd

    x_own, x_far, x_fwd = gather(x_ref, xs)
    g_own, g_far, g_fwd = gather(g_ref, gs)
    for c in x_far:
        c.start()
    x_own.start()
    g_own.start()
    for three in wcopies:
        three[2].start()

    decay = ld_ref[...]
    ti = lax.broadcasted_iota(jnp.int32, (rows, rows), 0)
    si_ = lax.broadcasted_iota(jnp.int32, (rows, rows), 1)
    lower = jnp.where(ti >= si_, 1.0, 0.0).astype(f32)
    eye = jnp.where(ti == si_, 1.0, 0.0).astype(f32)
    run_row = nt(decay, lower, HIGHEST)
    run_col = nt(lower, decay, HIGHEST)
    decay_col = nt(eye, decay, HIGHEST)
    inf_row = inflow_of(decay)
    for h in range(heads):
        run_r[h] = run_row[h : h + 1, :]
        inf_r[h] = inf_row[h : h + 1, :]
    col = lax.broadcasted_iota(jnp.int32, (heads, vwid), 1)
    first = lax.broadcasted_iota(jnp.int32, (heads, vwid), 0) * hdim
    spread = jnp.where((col >= first) & (col < first + hdim), 1.0, 0.0).astype(f32)
    run_x[...] = nn(run_col, spread, HIGHEST)
    ent_x[...] = nn(jnp.exp(run_col), spread, HIGHEST)
    to_end = jnp.exp(run_col[rows - 1 : rows, :] - run_col) * inflow_of(decay_col)
    end_x[...] = nn(to_end, spread, HIGHEST)

    sendd[...] = jnp.zeros(sendd.shape, f32)
    sendd[:, 0:heads] = jnp.broadcast_to(jnp.exp(run_col[rows - 1 : rows, :]), (8, heads))
    recvd[si] = sendd[...]
    d_copies = [
        remote(sendd, recvd.at[si], {"seq": lax.rem(si + o, n_seq)}) for o in range(1, n_seq)
    ]
    for c in d_copies:
        c.start()

    def mul_x(src, block, begin):
        @pl.loop(0, vwid // TILE)
        def _(n):
            at = pl.ds(pl.multiple_of(n * TILE, TILE), TILE)
            p = nn(block[...], vw[pl.ds(pl.multiple_of(src * width, width), width), at])
            acc_v[:, at] = p if begin else acc_v[:, at] + p

        @pl.loop(0, pwid // TILE)
        def _(n):
            at = pl.ds(pl.multiple_of(n * TILE, TILE), TILE)
            p = nn(block[...], sw[pl.ds(pl.multiple_of(src * width, width), width), at])
            acc_p[:, at] = p if begin else acc_p[:, at] + p

    def mul_g(src, block, begin):
        @pl.loop(0, vwid // TILE)
        def _(n):
            at = pl.ds(pl.multiple_of(n * TILE, TILE), TILE)
            p = nt(block[...], ow[at, pl.ds(pl.multiple_of(src * width, width), width)])
            acc_g[:, at] = p if begin else acc_g[:, at] + p

    wcopies[0][0].wait()
    wcopies[0][1].wait()
    x_here.wait()
    mul_x(hi, xs.at[hi], True)
    x_own.wait_recv()
    wcopies[1][0].wait()
    wcopies[1][1].wait()
    mul_x(partner, xs.at[partner], False)
    per = chips - 1
    for k in range(CHUNKS):
        for j in range(per):
            x_far[k * per + j].wait_recv()
            x_fwd[k * per + j].start()
            g_far[k * per + j].start()
    for j in range(per):
        src = at_chip(chips - 1 - j, core)
        for which in (0, 1):
            wcopies[2 + 2 * j + which][0].wait()
            wcopies[2 + 2 * j + which][1].wait()
        mul_x(src, xs.at[src], False)
        for k in range(CHUNKS):
            x_fwd[k * per + j].wait_recv()
        src = at_chip(chips - 1 - j, 1 - core)
        mul_x(src, xs.at[src], False)
    values[...] = acc_v[...].astype(bf16)
    pairs[...] = acc_p[...].astype(bf16)

    there, back = [], []
    for way in (0, 1):
        to = [lax.rem(si + o, n_seq) for o in range(1, n_seq)]
        there.append([remote(sendb.at[way, t], recvb.at[way, si], {"seq": t}) for t in to])
        back.append([remote(backb.at[way, t], backr.at[way, si], {"seq": t}) for t in to])

    def piece(r):
        row, col = (r % row_cuts) * prow, (r // row_cuts) * pcol
        return slice(row, row + prow), slice(col, col + pcol)

    def scan_begin(way):
        for r in range(n_seq):
            at = piece(r)
            sendb[way, r] = total[way, at[0], at[1]].astype(bf16)
        for c in there[way]:
            c.start()
        recvb[way, si] = sendb[way, si]

    def scan_mid(way):
        for c in there[way]:
            c.wait_recv()
        cols = pl.ds(pl.multiple_of((si // row_cuts) * pcol, 128), pcol)
        state = jnp.zeros((prow, pcol), f32)
        for q in range(n_seq) if way == 0 else range(n_seq - 1, -1, -1):
            backb[way, q] = state.astype(bf16)
            state = dec[q, 0:1, cols] * state + recvb[way, q].astype(f32)
        for c in back[way]:
            c.start()
        backr[way, si] = backb[way, si]

    def scan_end(way):
        for c in back[way]:
            c.wait_recv()
        for r in range(n_seq):
            at = piece(r)
            excl[way, at[0], at[1]] = backr[way, r]

    tv[...] = (end_x[...] * values[...].astype(f32)).astype(bf16)
    for g in range(groups):
        cols = slice(g * gwid, (g + 1) * gwid)
        w_at = slice(2 * g * STATE, (2 * g + 1) * STATE)
        total[0, :, cols] = tn(pairs[:, w_at], tv[:, cols])
    scan_begin(0)
    for c in d_copies:
        c.wait_recv()
    lane = lax.broadcasted_iota(jnp.int32, (128, vwid), 1)
    head = lax.broadcasted_iota(jnp.int32, (128, vwid), 0) * hdim
    widen = jnp.where((lane >= head) & (lane < head + hdim), 1.0, 0.0).astype(f32)
    wide = nn(recvd[...].reshape(n_seq * 8, 128), widen, HIGHEST)
    dec[...] = wide.reshape(n_seq, 8, vwid)
    for g in range(groups):
        w_at = slice(2 * g * STATE, (2 * g + 1) * STATE)
        r_at = slice((2 * g + 1) * STATE, (2 * g + 2) * STATE)
        score[g] = nt(pairs[:, r_at], pairs[:, w_at])
        dscore[g] = jnp.zeros((rows, rows), f32)

    wcopies[0][2].wait()
    g_here.wait()
    mul_g(hi, gs.at[hi], True)
    per_group = gwid // pair

    @pl.loop(0, heads // 2)
    def _(i):
        g = i // per_group
        at = pl.ds(pl.multiple_of(i * pair, pair), pair)
        left = lax.broadcasted_iota(jnp.int32, (rows, pair), 1) < hdim
        causal = lax.broadcasted_iota(jnp.int32, (rows, rows), 0) >= lax.broadcasted_iota(
            jnp.int32, (rows, rows), 1
        )
        vp = values[:, at]
        rx = run_x[:, at]
        s = score[g]
        gain = jnp.where(left, skip_ref[2 * i], skip_ref[2 * i + 1])
        outs = []
        for h in (0, 1):
            rc = rx[:, h * hdim : h * hdim + 1]
            m = jnp.exp(jnp.where(causal, rc - run_r[2 * i + h], -1e30)) * inf_r[2 * i + h]
            w = (s * m).astype(bf16)
            mask[2 * i + h] = m.astype(bf16)
            weight[2 * i + h] = w
            outs.append(nn(w, vp))
        acc_v[:, at] = jnp.where(left, outs[0], outs[1]) + gain * vp.astype(f32)

    g_own.wait_recv()
    wcopies[1][2].wait()
    mul_g(partner, gs.at[partner], False)
    scan_mid(0)
    for k in range(CHUNKS):
        for j in range(per):
            g_far[k * per + j].wait_recv()
            g_fwd[k * per + j].start()
    for j in range(per):
        src = at_chip(chips - 1 - j, core)
        for which in (0, 1):
            wcopies[2 + 2 * j + which][2].wait()
        mul_g(src, gs.at[src], False)
        for k in range(CHUNKS):
            g_fwd[k * per + j].wait_recv()
        src = at_chip(chips - 1 - j, 1 - core)
        mul_g(src, gs.at[src], False)
    mgrad[...] = acc_g[...].astype(bf16)
    eg[...] = (ent_x[...] * mgrad[...].astype(f32)).astype(bf16)
    for g in range(groups):
        cols = slice(g * gwid, (g + 1) * gwid)
        r_at = slice((2 * g + 1) * STATE, (2 * g + 2) * STATE)
        total[1, :, cols] = tn(pairs[:, r_at], eg[:, cols])
    scan_begin(1)

    def within_back():
        @pl.loop(0, heads // 2)
        def _(i):
            g = i // per_group
            at = pl.ds(pl.multiple_of(i * pair, pair), pair)
            left = lax.broadcasted_iota(jnp.int32, (rows, pair), 1) < hdim
            vp = values[:, at]
            gp = mgrad[:, at]
            gp32 = gp.astype(f32)
            gain = jnp.where(left, skip_ref[2 * i], skip_ref[2 * i + 1])
            grads, ds = [], None
            for h in (0, 1):
                grads.append(tn(weight[2 * i + h], gp))
                gh = jnp.where(left == (h == 0), gp32, 0.0).astype(bf16)
                d = mask[2 * i + h].astype(f32) * nt(gh, vp)
                ds = d if ds is None else ds + d
            acc_g[:, at] = jnp.where(left, grads[0], grads[1]) + gain * gp32
            dscore[g] = dscore[g] + ds

    scan_end(0)

    half = width // 2
    parts = (0, 1)

    def tiles(partial, dest, c, use):
        @pl.loop(0, half // TILE)
        def _(n):
            at = pl.ds(pl.multiple_of(n * TILE, TILE), TILE)
            use(at, partial(dest * width + c * half + n * TILE))

    def scatter_begin(u, partial):
        near = [
            [remote(p_send.at[u, j, c], p_recv.at[u, j, c], {"head": partner}) for c in parts]
            for j in range(per)
        ]
        far = [
            [
                remote(y_send.at[u, j, c], y_recv.at[u, j, c], {"head": at_chip(j + 1, core)})
                for c in parts
            ]
            for j in range(per)
        ]
        own = [remote(o_send.at[u, c], o_recv.at[u, c], {"head": partner}) for c in parts]
        for j in range(per):
            for c in parts:
                def keep(at, p):
                    p_send[u, j, c, :, at] = p.astype(bf16)

                tiles(partial, at_chip(j + 1, 1 - core), c, keep)
                near[j][c].start()
        for j in range(per):
            for c in parts:
                def keep_part(at, p):
                    part[u, c, :, at] = p

                tiles(partial, at_chip(j + 1, core), c, keep_part)
                near[j][c].wait_recv()
                y_send[u, j, c] = (part[u, c] + p_recv[u, j, c].astype(f32)).astype(bf16)
                far[j][c].start()
        for c in parts:
            def keep_own(at, p):
                o_send[u, c, :, at] = p.astype(bf16)

            tiles(partial, partner, c, keep_own)
            own[c].start()
        for c in parts:
            def keep_mine(at, p):
                part[u, c, :, at] = p

            tiles(partial, hi, c, keep_mine)
        return near, far, own

    def scatter_end(u, three, o_ref):
        near, far, own = three
        for c in parts:
            own[c].wait_recv()
            s = part[u, c] + o_recv[u, c].astype(f32)
            for j in range(per):
                far[j][c].wait_recv()
                s = s + y_recv[u, j, c].astype(f32)
            o_ref[:, c * half : (c + 1) * half] = s.astype(bf16)
        for c in parts:
            for copy in [n[c] for n in near] + [f[c] for f in far] + [own[c]]:
                copy.wait_send()

    for g in range(groups):
        cols = slice(g * gwid, (g + 1) * gwid)
        r_at = slice((2 * g + 1) * STATE, (2 * g + 2) * STATE)
        carried = ent_x[:, cols] * nn(pairs[:, r_at], excl[0, :, cols])
        mix[:, cols] = (acc_v[:, cols] + carried).astype(bf16)

    def out_partial(first_col):
        return nn(mix[...], ow[:, pl.ds(pl.multiple_of(first_col, TILE), TILE)])

    first_rs = scatter_begin(0, out_partial)

    within_back()
    scan_mid(1)
    scan_end(1)
    for g in range(groups):
        cols = slice(g * gwid, (g + 1) * gwid)
        w_at = slice(2 * g * STATE, (2 * g + 1) * STATE)
        r_at = slice((2 * g + 1) * STATE, (2 * g + 2) * STATE)
        inc = excl[0, :, cols]
        outg = excl[1, :, cols]
        dval[:, cols] = (acc_g[:, cols] + end_x[:, cols] * nn(pairs[:, w_at], outg)).astype(bf16)
        ds = dscore[g].astype(bf16)
        dpair[:, w_at] = (tn(ds, pairs[:, r_at]) + nt(tv[:, cols], outg)).astype(bf16)
        dpair[:, r_at] = (nn(ds, pairs[:, w_at]) + nt(eg[:, cols], inc)).astype(bf16)

    def in_partial(first_row):
        at = pl.ds(pl.multiple_of(first_row, TILE), TILE)
        return nt(dval[...], vw[at, :]) + nt(dpair[...], sw[at, :])

    second_rs = scatter_begin(1, in_partial)
    scatter_end(0, first_rs, out_ref)
    scatter_end(1, second_rs, ing_ref)

    for c in [x_own, g_own] + x_far + x_fwd + g_far + g_fwd:
        c.wait_send()
    for c in d_copies + there[0] + there[1] + back[0] + back[1]:
        c.wait_send()


def place(a_ref, b_ref, a_out, b_out, sem):
    first = pltpu.make_async_copy(a_ref, a_out, sem.at[0])
    second = pltpu.make_async_copy(b_ref, b_out, sem.at[1])
    first.start()
    second.start()
    first.wait()
    second.wait()


def per_device(
    n_head, n_seq,
    layer_input, value_weight, state_weight, output_weight, log_decay, skip_gain, output_grad,
):
    rows, width = layer_input.shape
    full, vwid = value_weight.shape
    pwid = state_weight.shape[1]
    heads = log_decay.shape[0]
    groups = pwid // (2 * STATE)
    row_cuts = min(n_seq, STATE // 16)
    piece = (n_seq, STATE // row_cuts, vwid // (n_seq // row_cuts))
    sems = 32 * n_head + 5 * n_seq
    chips = n_head // 2
    per = max(chips - 1, 1)
    vm = pltpu.VMEM
    scratch = [
        vm((full, vwid), bf16), vm((full, pwid), bf16), vm((vwid, full), bf16),
        vm((n_head, rows, width), bf16), vm((n_head, rows, width), bf16),
        vm((rows, vwid), f32), vm((rows, pwid), f32), vm((rows, vwid), f32),
        vm((rows, vwid), bf16), vm((rows, pwid), bf16), vm((rows, vwid), bf16),
        vm((rows, vwid), bf16), vm((rows, vwid), bf16), vm((rows, pwid), bf16),
        vm((rows, vwid), f32), vm((rows, vwid), f32), vm((rows, vwid), f32),
        vm((heads, 1, rows), f32), vm((heads, 1, rows), f32),
        vm((groups, rows, rows), f32), vm((groups, rows, rows), f32),
        vm((rows, vwid), bf16), vm((rows, vwid), bf16),
        vm((2, STATE, vwid), f32), vm((2, STATE, vwid), bf16),
        vm((2,) + piece, bf16), vm((2,) + piece, bf16),
        vm((2,) + piece, bf16), vm((2,) + piece, bf16),
        vm((8, 128), f32), vm((n_seq, 8, 128), f32), vm((n_seq, 8, vwid), f32),
        vm((2, per, 2, rows, width // 2), bf16), vm((2, per, 2, rows, width // 2), bf16),
        vm((2, per, 2, rows, width // 2), bf16), vm((2, per, 2, rows, width // 2), bf16),
        vm((2, 2, rows, width // 2), bf16), vm((2, 2, rows, width // 2), bf16),
        vm((2, 2, rows, width // 2), f32),
        vm((heads, rows, rows), bf16), vm((heads, rows, rows), bf16),
        pltpu.SemaphoreType.DMA((sems,)),
        pltpu.SemaphoreType.DMA((sems,)),
        pltpu.SemaphoreType.DMA((3 * n_head + 2,)),
    ]
    vspec = pl.BlockSpec(memory_space=vm)
    anys = pl.BlockSpec(memory_space=pl.ANY)
    flops = 2 * rows * full * (3 * vwid + pwid) + 2 * rows * full * (vwid + pwid)
    made = pl.pallas_call(
        functools.partial(kernel, n_head, n_seq),
        out_shape=(
            jax.ShapeDtypeStruct((rows, width), bf16),
            jax.ShapeDtypeStruct((rows, width), bf16),
        ),
        in_specs=[anys, anys, vspec, pl.BlockSpec(memory_space=pltpu.SMEM), anys, anys, anys],
        out_specs=(vspec, vspec),
        scratch_shapes=scratch,
        compiler_params=pltpu.CompilerParams(
            collective_id=0, has_side_effects=True, vmem_limit_bytes=60 * 2**20
        ),
        cost_estimate=pl.CostEstimate(
            flops=flops, bytes_accessed=2 * full * (2 * vwid + pwid), transcendentals=0
        ),
    )(layer_input, output_grad, log_decay, skip_gain, value_weight, state_weight, output_weight)
    return pl.pallas_call(
        place,
        out_shape=tuple(jax.ShapeDtypeStruct(a.shape, a.dtype) for a in made),
        in_specs=[anys, anys],
        out_specs=(anys, anys),
        scratch_shapes=[pltpu.SemaphoreType.DMA((2,))],
    )(*made)


def solution(mesh):
    from jax.sharding import PartitionSpec as P

    in_specs = (
        P("seq", "head"),
        P(None, "head"),
        P(None, "head"),
        P("head", None),
        P("head", "seq"),
        P("head"),
        P("seq", "head"),
    )
    out_specs = (P("seq", "head"), P("seq", "head"))
    return jax.shard_map(
        functools.partial(per_device, mesh.shape["head"], mesh.shape["seq"]),
        mesh=mesh, in_specs=in_specs, out_specs=out_specs, check_vma=False,
    )
```
